32 devices in a mesh: tm: 4 (over y, x), space: 8 (over z, core).
Axes of the slice: x: 2, y: 2, z: 4, core: 2. Of those that a mesh axis runs over, the one named last changes fastest.
Arguments:
- initial: float32 [32, 128, 128], P('space'), may hold values from -6 to 6
- guess: float32 [4, 32, 128, 128], P('tm', 'space'), may hold values from -6 to 6
- velocity: float32 [4, 3, 32, 128, 128], P(None, None, 'space'), may hold values from -0.6 to 0.6
- heat_shape: float32 [32, 128, 128], P('space'), may hold values from 0.002 to 0.02
- rack_map: int32 [32, 128], P('space'), may hold values from 0 to 63
- power: int32 [64, 64], P('tm'), may hold values from 0 to 7
- fan_mode: int32 [64], replicated, may hold values from 0 to 3
Outputs:
- states: float32 [64, 32, 128, 128], P('tm', 'space')
The draws below stay inside these ranges and needn't reach their ends.
All inputs are finite; a program needn't handle non-finite values.
Results may differ from the reference program's by a relative error of at most 0.00029.
Values sent between devices are 32-bit elements; how exact they have to be, the bound alone decides.
A program may use at most 64 MiB of HBM per device.

```python
import math
import jax
import jax.numpy as jnp

NY = 128
NZ = 128
STEP_DEV = 16
SWEEPS = 2
NFAN = 4
RACKS = 64
LEVELS = 8
NX = 32
STEPS = 64
N_TM = 4


def plant(result, stream_key, smallest, top_value):
    longest = result.shape.index(max(result.shape))
    spots = []
    for shift in (0, 1):
        where = [jax.random.randint(jax.random.fold_in(stream_key, axis), (), 0, length) for axis, length in enumerate(result.shape)]
        where[longest] = (where[longest] + shift) % result.shape[longest]
        spots.append(tuple(where))
    return result.at[spots[0]].set(smallest).at[spots[1]].set(top_value)


def shard_levels(stream_key, dims, shards, smallest, largest):
    factor_of = 1.0
    for position, shards_of in shards:
        steps = jax.random.uniform(jax.random.fold_in(jax.random.fold_in(stream_key, 6), position), (shards_of,), jnp.float32, smallest / len(shards), largest / len(shards))
        factor_of = factor_of * jnp.repeat(jnp.exp(steps), dims[position] // shards_of).reshape((-1,) + (1,) * (len(dims) - 1 - position))
    return factor_of


def scatter_about(stream_key, extent, spread, reach, cuts=(), kind=jnp.bfloat16):
    array = spread * jax.random.normal(stream_key, extent, jnp.float32)
    if cuts:
        array = array * shard_levels(stream_key, extent, cuts, -0.22, 0.18)
    return jnp.clip(array, -reach, reach).astype(kind)


def setup_inputs(seed: int = 0) -> dict:
    keys = jax.random.split(jax.random.key(seed), 8)
    return {
        "initial": scatter_about(keys[0], (NX, NY, NZ), 1.0, 6.0, ((0, 8),), jnp.float32),
        "guess": scatter_about(keys[1], (N_TM, NX, NY, NZ), 1.0, 6.0, ((0, 4), (1, 8)), jnp.float32),
        "velocity": scatter_about(keys[2], (NFAN, 3, NX, NY, NZ), 0.15, 0.6, ((2, 8),), jnp.float32),
        "heat_shape": jnp.clip(jnp.exp(math.log(0.02) - 2.30258502 * jax.random.uniform(keys[3], (NX, NY, NZ), jnp.float32) ** shard_levels(keys[3], (NX, NY, NZ), ((0, 8),), -0.2, 0.2)), 0.002, 0.02),
        "rack_map": plant(jax.random.randint(keys[4], (NX, NY), 0, RACKS), jax.random.fold_in(keys[4], 1), 0, RACKS - 1).astype(jnp.int32),
        "power": plant(jax.random.randint(keys[5], (STEPS, RACKS), 0, LEVELS), jax.random.fold_in(keys[5], 1), 0, LEVELS - 1).astype(jnp.int32),
        "fan_mode": plant(jax.random.randint(keys[6], (STEPS,), 0, NFAN), jax.random.fold_in(keys[6], 1), 0, NFAN - 1).astype(jnp.int32),
    }


DIFFUSE = 0.5


def jacobi_sweep(current, source, courant, scale_ratio):
    diffusion = DIFFUSE * scale_ratio
    half_ratio = 0.5 * scale_ratio
    padded = jnp.pad(current, 1)
    summed = source + (diffusion - half_ratio * courant[0]) * padded[2:, 1:-1, 1:-1] + (diffusion + half_ratio * courant[0]) * padded[:-2, 1:-1, 1:-1]
    summed = summed + (diffusion - half_ratio * courant[1]) * padded[1:-1, 2:, 1:-1] + (diffusion + half_ratio * courant[1]) * padded[1:-1, :-2, 1:-1]
    summed = summed + (diffusion - half_ratio * courant[2]) * padded[1:-1, 1:-1, 2:] + (diffusion + half_ratio * courant[2]) * padded[1:-1, 1:-1, :-2]
    return summed / (1.0 + 6.0 * diffusion)


def implicit_solve(first_state, source, courant, scale_ratio):
    current = first_state
    for sweep_index in range(SWEEPS):
        current = jacobi_sweep(current, source, courant, scale_ratio)
    return current


def reference(initial, guess, velocity, heat_shape, rack_map, power, fan_mode):
    def advance(current, step_index):
        heat_now = heat_shape * power[step_index][rack_map].astype(jnp.float32)[:, :, None]
        return implicit_solve(current, current + heat_now, velocity[fan_mode[step_index]], 1.0)

    residuals = []
    for block_index in range(N_TM):
        current = initial if block_index == 0 else guess[block_index - 1]
        for offset in range(STEP_DEV):
            current = advance(current, block_index * STEP_DEV + offset)
        residuals.append(current - guess[block_index])
    corrected = []
    correction = residuals[0]
    for block_index in range(N_TM):
        if block_index > 0:
            courant = velocity[fan_mode[block_index * STEP_DEV + STEP_DEV - 1]]
            correction = implicit_solve(correction, correction, courant, float(STEP_DEV)) + residuals[block_index]
        corrected.append(guess[block_index] + correction)
    results = []
    for block_index in range(N_TM):
        current = initial if block_index == 0 else corrected[block_index - 1]
        for offset in range(STEP_DEV - 1):
            current = advance(current, block_index * STEP_DEV + offset)
            results.append(current)
        results.append(corrected[block_index])
    return jnp.stack(results)
```

```python
import functools

import jax
import jax.numpy as jnp
from jax import lax
from jax.experimental import pallas as pl
from jax.experimental.pallas import tpu as pltpu
from jax.sharding import PartitionSpec as P

PAD = 8
CHUNK = 32
MESH = pl.DeviceIdType.MESH


def padded_1(x):
    peers, length = (lax.axis_size("space"), x.shape[0])
    up = [(i, i + 1) for i in range(peers - 1)]
    down = [(i + 1, i) for i in range(peers - 1)]
    before = lax.ppermute(x[length - 1 :], "space", up)
    after = lax.ppermute(x[:1], "space", down)
    return jnp.concatenate([before, x, after], axis=0)


def kernel(
    blocks, slabs, fan, initial, guess, velocity, heat, states,
    cur, mid, inc, start, own_guess, residual, corr, vel,
    halo_send, halo_recv, inc_send, inc_recv, vel_send, vel_recv,
    tm_send, tm_recv, local_sem,
):
    steps = states.shape[0]
    planes, ny, nz = initial.shape
    rows = pl.ds(PAD, ny)
    k = lax.axis_index("tm")
    j = lax.axis_index("space")
    has_left, has_right = j > 0, j < slabs - 1
    has_before, has_after = k > 0, k < blocks - 1
    sides = ((0, has_left, j - 1), (1, has_right, j + 1))

    cur[...] = jnp.zeros_like(cur)
    mid[...] = jnp.zeros_like(mid)
    inc[...] = jnp.zeros_like(inc)
    for edge in (0, planes + 1):
        for mode in range(vel.shape[0]):
            vel[mode, :, edge] = jnp.zeros((3, ny, nz), jnp.float32)

    barrier = pltpu.get_barrier_semaphore()
    greet = (
        (has_left, {"space": j - 1}), (has_right, {"space": j + 1}),
        (has_before, {"tm": k - 1}), (has_after, {"tm": k + 1}),
    )
    for there, who in greet:
        @pl.when(there)
        def _():
            pl.semaphore_signal(barrier, inc=1, device_id=who, device_id_type=MESH)
    pl.semaphore_wait(barrier, sum(there.astype(jnp.int32) for there, who in greet))

    def edges_of(side, width, first):
        if side == 0:
            return pl.ds(first, width), pl.ds(first + planes, width)
        return pl.ds(first + planes - width, width), pl.ds(first - width, width)

    def edge_copy(side, peer, buffer, send, recv):
        here, there = edges_of(side, 2, 2)
        return pltpu.make_async_remote_copy(
            src_ref=buffer.at[here, rows], dst_ref=buffer.at[there, rows],
            send_sem=send, recv_sem=recv,
            device_id={"space": peer}, device_id_type=MESH,
        )

    def vel_copy(side, peer):
        here, there = edges_of(side, 1, 1)
        here = pl.ds(0, 1) if side == 0 else pl.ds(planes - 1, 1)
        return pltpu.make_async_remote_copy(
            src_ref=velocity.at[:, :, here], dst_ref=vel.at[:, :, there],
            send_sem=vel_send.at[side], recv_sem=vel_recv.at[1 - side],
            device_id={"space": peer}, device_id_type=MESH,
        )

    def both(copy_of, act):
        for side, there, peer in sides:
            @pl.when(there)
            def _():
                act(side, copy_of(side, peer))

    def begin(side, copy):
        copy.start()

    def end(recv_of):
        def act(side, copy):
            copy.wait_send()
        return act

    own = pl.ds(2, planes)
    guess_copy = pltpu.make_async_remote_copy(
        src_ref=guess.at[0], dst_ref=cur.at[0, own, rows],
        send_sem=tm_send.at[0], recv_sem=tm_recv.at[0],
        device_id={"tm": k + 1}, device_id_type=MESH,
    )
    corr_copy = pltpu.make_async_remote_copy(
        src_ref=corr, dst_ref=inc.at[own, rows],
        send_sem=tm_send.at[1], recv_sem=tm_recv.at[1],
        device_id={"tm": k + 1}, device_id_type=MESH,
    )

    @pl.when(has_after)
    def _():
        guess_copy.start()

    both(vel_copy, begin)
    vel_in = pltpu.make_async_copy(velocity, vel.at[:, :, pl.ds(1, planes)], local_sem.at[0])
    vel_in.start()
    guess_in = pltpu.make_async_copy(guess.at[0], own_guess, local_sem.at[1])
    guess_in.start()

    @pl.when(jnp.logical_not(has_before))
    def _():
        first_in = pltpu.make_async_copy(initial, cur.at[0, own, rows], local_sem.at[2])
        first_in.start()
        first_in.wait()

    @pl.when(has_before)
    def _():
        guess_copy.wait_recv()

    def cur_copy(slot):
        def make(side, peer):
            return edge_copy(
                side, peer, cur.at[slot], halo_send.at[slot, side], halo_recv.at[slot, 1 - side]
            )
        return make

    def inc_copy(side, peer):
        return edge_copy(side, peer, inc, inc_send.at[side], inc_recv.at[1 - side])

    def wait_edges(make):
        for side, there, peer in sides:
            @pl.when(there)
            def _():
                make(side, peer).wait_send()
                make(1 - side, peer).wait_recv()

    both(cur_copy(0), begin)
    vel_in.wait()
    guess_in.wait()
    for side, there, peer in sides:
        @pl.when(there)
        def _():
            vel_copy(side, peer).wait_send()
            vel_copy(1 - side, peer).wait_recv()
    wait_edges(cur_copy(0))

    lane = lax.broadcasted_iota(jnp.int32, (CHUNK, nz), 1)
    low, high = lane == 0, lane == nz - 1

    def sweep(read, source, fan_index, vel_plane, ratio, scale, store):
        half = 0.5 * ratio
        for at in range(0, ny, CHUNK):
            here = pl.ds(PAD + at, CHUNK)
            tile = pl.ds(at, CHUNK)
            centre = read(1, here)
            after, before = read(2, here), read(0, here)
            total = after + before
            drift = vel[fan_index, 0, vel_plane, tile] * (after - before)
            after = read(1, pl.ds(PAD + at + 1, CHUNK))
            before = read(1, pl.ds(PAD + at - 1, CHUNK))
            total = total + (after + before)
            drift = drift + vel[fan_index, 1, vel_plane, tile] * (after - before)
            after = jnp.where(high, 0.0, pltpu.roll(centre, nz - 1, 1))
            before = jnp.where(low, 0.0, pltpu.roll(centre, 1, 1))
            total = total + (after + before)
            drift = drift + vel[fan_index, 2, vel_plane, tile] * (after - before)
            store(tile, here, (source(tile, here) + half * (total - drift)) * scale)

    def first_sweep(wide, fan_index, ratio, heat_of):
        inverse = 1.0 / (1.0 + 3.0 * ratio)

        def plane(i, carry):
            off = jnp.logical_or(
                jnp.logical_and(i == 0, j == 0),
                jnp.logical_and(i == planes + 1, j == slabs - 1),
            )
            scale = jnp.where(off, 0.0, inverse).astype(jnp.float32)

            def source(tile, here):
                value = wide[i + 1, here]
                return value if heat_of is None else value + heat_of(i, tile)

            def store(tile, here, value):
                mid[i, here] = value

            sweep(lambda d, at: wide[i + d, at], source, fan_index, i, ratio, scale, store)
            return carry

        lax.fori_loop(0, planes + 2, plane, 0)

    def second_sweep(wide, fan_index, ratio, heat_of, put):
        inverse = 1.0 / (1.0 + 3.0 * ratio)

        def plane(i, carry):
            def source(tile, here):
                value = wide[i + 2, here]
                return value if heat_of is None else value + heat_of(i + 1, tile)

            sweep(
                lambda d, at: mid[i + d, at], source, fan_index, i + 1, ratio, inverse,
                lambda tile, here, value: put(i, tile, here, value),
            )
            return carry

        lax.fori_loop(0, planes, plane, 0)

    def step(s, keep, more):
        slot = lax.rem(s, 2)
        other = 1 - slot

        @pl.when(s > 0)
        def _():
            wait_edges(cur_copy(slot))

        fan_index = fan[k * steps + s]
        wide = cur.at[slot]

        def heat_of(i, tile):
            return heat[s, i, tile]

        def put(i, tile, here, value):
            cur[other, i + 2, here] = value
            if keep:
                states[s, i, tile] = value

        first_sweep(wide, fan_index, 1.0, heat_of)
        second_sweep(wide, fan_index, 1.0, heat_of, put)

        @pl.when(more)
        def _():
            both(cur_copy(other), begin)

    start[...] = cur[0]

    def pass_one(s, carry):
        step(s, False, s < steps - 1)
        return carry

    lax.fori_loop(0, steps, pass_one, 0)
    for i in range(planes):
        residual[i] = cur[steps % 2, i + 2, rows] - own_guess[i]

    @pl.when(has_before)
    def _():
        corr_copy.wait_recv()

    both(inc_copy, begin)
    wait_edges(inc_copy)

    coarse_fan = fan[k * steps + steps - 1]
    coarse = float(steps)

    def put_corr(i, tile, here, value):
        value = value + residual[i, tile]
        corr[i, tile] = value
        states[steps - 1, i, tile] = own_guess[i, tile] + value

    first_sweep(inc, coarse_fan, coarse, None)
    second_sweep(inc, coarse_fan, coarse, None, put_corr)

    @pl.when(has_after)
    def _():
        corr_copy.start()

    cur[0] = start[...] + inc[...]

    def pass_two(s, carry):
        step(s, True, s < steps - 2)
        return carry

    lax.fori_loop(0, steps - 1, pass_two, 0)

    @pl.when(has_after)
    def _():
        guess_copy.wait_send()
        corr_copy.wait_send()


def local(initial, guess, velocity, heat_shape, rack_map, power, fan_mode):
    blocks, slabs = lax.axis_size("tm"), lax.axis_size("space")
    planes, ny, nz = initial.shape
    steps, racks = power.shape
    rack_wide = padded_1(rack_map)
    heat_wide = padded_1(heat_shape)
    onehot = (rack_wide[:, :, None] == lax.iota(jnp.int32, racks)[None, None, :]).astype(jnp.float32)
    cell_power = jnp.einsum(
        "xyr,kr->kxy", onehot, power.astype(jnp.float32), precision=lax.Precision.HIGHEST
    )
    heat = heat_wide[None] * cell_power[:, :, :, None]
    tall = ny + 2 * PAD
    vmem = pl.BlockSpec(memory_space=pltpu.VMEM)
    hbm = pl.BlockSpec(memory_space=pl.ANY)
    f32 = jnp.float32
    return pl.pallas_call(
        functools.partial(kernel, blocks, slabs),
        out_shape=jax.ShapeDtypeStruct((steps, planes, ny, nz), f32),
        in_specs=[pl.BlockSpec(memory_space=pltpu.SMEM), hbm, hbm, hbm, vmem],
        out_specs=vmem,
        scratch_shapes=[
            pltpu.VMEM((2, planes + 4, tall, nz), f32),
            pltpu.VMEM((planes + 2, tall, nz), f32),
            pltpu.VMEM((planes + 4, tall, nz), f32),
            pltpu.VMEM((planes + 4, tall, nz), f32),
            pltpu.VMEM((planes, ny, nz), f32),
            pltpu.VMEM((planes, ny, nz), f32),
            pltpu.VMEM((planes, ny, nz), f32),
            pltpu.VMEM((velocity.shape[0], 3, planes + 2, ny, nz), f32),
            pltpu.SemaphoreType.DMA((2, 2)),
            pltpu.SemaphoreType.DMA((2, 2)),
            pltpu.SemaphoreType.DMA((2,)),
            pltpu.SemaphoreType.DMA((2,)),
            pltpu.SemaphoreType.DMA((2,)),
            pltpu.SemaphoreType.DMA((2,)),
            pltpu.SemaphoreType.DMA((2,)),
            pltpu.SemaphoreType.DMA((2,)),
            pltpu.SemaphoreType.DMA((3,)),
        ],
        compiler_params=pltpu.CompilerParams(
            collective_id=0, has_side_effects=True, vmem_limit_bytes=40 * 1024 * 1024
        ),
    )(fan_mode, initial, guess, velocity, heat)


def solution(mesh):
    placed = (
        P("space", None, None),
        P("tm", "space", None, None),
        P(None, None, "space", None, None),
        P("space", None, None),
        P("space", None),
        P("tm", None),
        P(),
    )
    return jax.shard_map(
        local, mesh=mesh, in_specs=placed, out_specs=P("tm", "space", None, None), check_vma=False
    )
```

```python
import functools

import jax
import jax.numpy as jnp
from jax import lax
from jax.experimental import pallas as pl
from jax.experimental.pallas import tpu as pltpu
from jax.sharding import PartitionSpec as P

PAD = 8
PARTS = 4
MESH = pl.DeviceIdType.MESH


def kernel(
    blocks, slabs, fan, initial, guess, velocity, shape_own, onehot_own, levels, states,
    heat, shape_wide, onehot, cur, mid, inc, start, own_guess, residual, corr, vel,
    halo_send, halo_recv, inc_send, inc_recv, vel_send, vel_recv,
    shape_send, shape_recv, onehot_send, onehot_recv,
    tm_send, tm_recv, local_sem,
):
    steps = states.shape[0]
    planes, ny, nz = initial.shape
    rows = pl.ds(PAD, ny)
    chunk = ny // PARTS
    halves = ((0, pl.ds(PAD, ny // 2)), (1, pl.ds(PAD + ny // 2, ny // 2)))
    k = lax.axis_index("tm")
    j = lax.axis_index("space")
    has_left, has_right = j > 0, j < slabs - 1
    has_before, has_after = k > 0, k < blocks - 1
    sides = ((0, has_left, j - 1), (1, has_right, j + 1))

    cur[...] = jnp.zeros_like(cur)
    mid[...] = jnp.zeros_like(mid)
    inc[...] = jnp.zeros_like(inc)
    for edge in (0, planes + 1):
        for mode in range(vel.shape[0]):
            vel[mode, :, edge] = jnp.zeros((3, ny, nz), jnp.float32)
        shape_wide[edge] = jnp.zeros((ny, nz), jnp.float32)
        onehot[edge] = jnp.zeros(onehot.shape[1:], jnp.float32)

    barrier = pltpu.get_barrier_semaphore()
    greet = (
        (has_left, {"space": j - 1}), (has_right, {"space": j + 1}),
        (has_before, {"tm": k - 1}), (has_after, {"tm": k + 1}),
    )
    for there, who in greet:
        @pl.when(there)
        def _():
            pl.semaphore_signal(barrier, inc=1, device_id=who, device_id_type=MESH)
    pl.semaphore_wait(barrier, sum(there.astype(jnp.int32) for there, who in greet))

    def edges_of(side, width, first):
        if side == 0:
            return pl.ds(first, width), pl.ds(first + planes, width)
        return pl.ds(first + planes - width, width), pl.ds(first - width, width)

    def edge_copy(side, peer, buffer, send, recv, rows=rows):
        here, there = edges_of(side, 2, 2)
        return pltpu.make_async_remote_copy(
            src_ref=buffer.at[here, rows], dst_ref=buffer.at[there, rows],
            send_sem=send, recv_sem=recv,
            device_id={"space": peer}, device_id_type=MESH,
        )

    def vel_copy(side, peer):
        here, there = edges_of(side, 1, 1)
        here = pl.ds(0, 1) if side == 0 else pl.ds(planes - 1, 1)
        return pltpu.make_async_remote_copy(
            src_ref=velocity.at[:, :, here], dst_ref=vel.at[:, :, there],
            send_sem=vel_send.at[side], recv_sem=vel_recv.at[1 - side],
            device_id={"space": peer}, device_id_type=MESH,
        )

    def plane_copy(source, wide, send, recv):
        def make(side, peer):
            here, there = edges_of(side, 1, 1)
            here = pl.ds(0, 1) if side == 0 else pl.ds(planes - 1, 1)
            return pltpu.make_async_remote_copy(
                src_ref=source.at[here], dst_ref=wide.at[there],
                send_sem=send.at[side], recv_sem=recv.at[1 - side],
                device_id={"space": peer}, device_id_type=MESH,
            )
        return make

    shape_copy = plane_copy(shape_own, shape_wide, shape_send, shape_recv)
    onehot_copy = plane_copy(onehot_own, onehot, onehot_send, onehot_recv)

    def both(copy_of, act):
        for side, there, peer in sides:
            @pl.when(there)
            def _():
                act(side, copy_of(side, peer))

    def begin(side, copy):
        copy.start()

    own = pl.ds(2, planes)
    guess_copy = pltpu.make_async_remote_copy(
        src_ref=guess.at[0], dst_ref=cur.at[0, own, rows],
        send_sem=tm_send.at[0], recv_sem=tm_recv.at[0],
        device_id={"tm": k + 1}, device_id_type=MESH,
    )
    corr_copy = pltpu.make_async_remote_copy(
        src_ref=corr, dst_ref=inc.at[own, rows],
        send_sem=tm_send.at[1], recv_sem=tm_recv.at[1],
        device_id={"tm": k + 1}, device_id_type=MESH,
    )

    @pl.when(has_after)
    def _():
        guess_copy.start()

    both(shape_copy, begin)
    both(onehot_copy, begin)
    both(vel_copy, begin)
    vel_in = pltpu.make_async_copy(velocity, vel.at[:, :, pl.ds(1, planes)], local_sem.at[0])
    vel_in.start()
    guess_in = pltpu.make_async_copy(guess.at[0], own_guess, local_sem.at[1])
    guess_in.start()

    middle = pl.ds(1, planes)
    shape_in = pltpu.make_async_copy(shape_own, shape_wide.at[middle], local_sem.at[3])
    shape_in.start()
    onehot_in = pltpu.make_async_copy(onehot_own, onehot.at[middle], local_sem.at[4])
    onehot_in.start()

    @pl.when(jnp.logical_not(has_before))
    def _():
        first_in = pltpu.make_async_copy(initial, cur.at[0, own, rows], local_sem.at[2])
        first_in.start()
        first_in.wait()

    @pl.when(has_before)
    def _():
        guess_copy.wait_recv()

    def cur_copy(slot, half):
        def make(side, peer):
            return edge_copy(
                side, peer, cur.at[slot], halo_send.at[slot, side, half],
                halo_recv.at[slot, 1 - side, half], halves[half][1],
            )
        return make

    def inc_copy(side, peer):
        return edge_copy(side, peer, inc, inc_send.at[side], inc_recv.at[1 - side])

    def wait_edges(make):
        for side, there, peer in sides:
            @pl.when(there)
            def _():
                make(side, peer).wait_send()
                make(1 - side, peer).wait_recv()

    for half in range(2):
        both(cur_copy(0, half), begin)
    vel_in.wait()
    guess_in.wait()
    shape_in.wait()
    onehot_in.wait()
    wait_edges(shape_copy)
    wait_edges(onehot_copy)

    def heat_step(s, carry):
        for i in range(planes + 2):
            picked = jnp.dot(onehot[i], levels[s], preferred_element_type=jnp.float32)
            heat[s, i] = shape_wide[i] * picked
        return carry

    lax.fori_loop(0, steps, heat_step, 0)
    wait_edges(vel_copy)
    for half in range(2):
        wait_edges(cur_copy(0, half))

    lane = lax.broadcasted_iota(jnp.int32, (chunk, nz), 1)
    low, high = lane == 0, lane == nz - 1

    def sweep(parts, read, source, fan_index, vel_plane, ratio, scale, store):
        half = 0.5 * ratio
        for at in (part * chunk for part in parts):
            here = pl.ds(PAD + at, chunk)
            tile = pl.ds(at, chunk)
            centre = read(1, here)
            after, before = read(2, here), read(0, here)
            total = after + before
            drift = vel[fan_index, 0, vel_plane, tile] * (after - before)
            after = read(1, pl.ds(PAD + at + 1, chunk))
            before = read(1, pl.ds(PAD + at - 1, chunk))
            total = total + (after + before)
            drift = drift + vel[fan_index, 1, vel_plane, tile] * (after - before)
            after = jnp.where(high, 0.0, pltpu.roll(centre, nz - 1, 1))
            before = jnp.where(low, 0.0, pltpu.roll(centre, 1, 1))
            total = total + (after + before)
            drift = drift + vel[fan_index, 2, vel_plane, tile] * (after - before)
            store(tile, here, (source(tile, here) + half * (total - drift)) * scale)

    def first_sweep(parts, which, wide, fan_index, ratio, heat_of):
        inverse = 1.0 / (1.0 + 3.0 * ratio)

        count, index_of = which

        def plane(turn, carry):
            i = index_of(turn)
            off = jnp.logical_or(
                jnp.logical_and(i == 0, j == 0),
                jnp.logical_and(i == planes + 1, j == slabs - 1),
            )
            scale = jnp.where(off, 0.0, inverse).astype(jnp.float32)

            def source(tile, here):
                value = wide[i + 1, here]
                return value if heat_of is None else value + heat_of(i, tile)

            def store(tile, here, value):
                mid[i, here] = value

            sweep(parts, lambda d, at: wide[i + d, at], source, fan_index, i, ratio, scale, store)
            return carry

        lax.fori_loop(0, count, plane, 0)

    def second_sweep(parts, wide, fan_index, ratio, heat_of, put):
        inverse = 1.0 / (1.0 + 3.0 * ratio)

        def plane(i, carry):
            def source(tile, here):
                value = wide[i + 2, here]
                return value if heat_of is None else value + heat_of(i + 1, tile)

            sweep(
                parts, lambda d, at: mid[i + d, at], source, fan_index, i + 1, ratio, inverse,
                lambda tile, here, value: put(i, tile, here, value),
            )
            return carry

        lax.fori_loop(0, planes, plane, 0)

    every = range(PARTS)
    front, back = range(PARTS // 2), range(PARTS // 2, PARTS)
    all_planes = (planes + 2, lambda turn: turn)
    inner = (planes - 2, lambda turn: turn + 2)
    outer = (4, lambda turn: turn + turn // 2 * (planes - 2))

    def step(s, keep, more):
        slot = lax.rem(s, 2)
        other = 1 - slot

        fan_index = fan[k * steps + s]
        wide = cur.at[slot]

        def heat_of(i, tile):
            return heat[s, i, tile]

        def put(i, tile, here, value):
            cur[other, i + 2, here] = value
            if keep:
                states[s, i, tile] = value

        def arrived(half):
            @pl.when(s > 0)
            def _():
                wait_edges(cur_copy(slot, half))

        def leave(half):
            @pl.when(more)
            def _():
                both(cur_copy(other, half), begin)

        first_sweep(every, inner, wide, fan_index, 1.0, heat_of)
        arrived(0)
        first_sweep((0,), outer, wide, fan_index, 1.0, heat_of)
        arrived(1)
        first_sweep((1, 2), outer, wide, fan_index, 1.0, heat_of)
        second_sweep(front, wide, fan_index, 1.0, heat_of, put)
        leave(0)
        first_sweep((3,), outer, wide, fan_index, 1.0, heat_of)
        second_sweep(back, wide, fan_index, 1.0, heat_of, put)
        leave(1)

    start[...] = cur[0]

    def pass_one(s, carry):
        step(s, False, s < steps - 1)
        return carry

    lax.fori_loop(0, steps, pass_one, 0)
    for i in range(planes):
        residual[i] = cur[steps % 2, i + 2, rows] - own_guess[i]

    @pl.when(has_before)
    def _():
        corr_copy.wait_recv()

    both(inc_copy, begin)
    wait_edges(inc_copy)

    coarse_fan = fan[k * steps + steps - 1]
    coarse = float(steps)

    def put_corr(i, tile, here, value):
        value = value + residual[i, tile]
        corr[i, tile] = value
        states[steps - 1, i, tile] = own_guess[i, tile] + value

    first_sweep(every, all_planes, inc, coarse_fan, coarse, None)
    second_sweep(every, inc, coarse_fan, coarse, None, put_corr)

    @pl.when(has_after)
    def _():
        corr_copy.start()

    cur[0] = start[...] + inc[...]

    def pass_two(s, carry):
        step(s, True, s < steps - 2)
        return carry

    lax.fori_loop(0, steps - 1, pass_two, 0)

    @pl.when(has_after)
    def _():
        guess_copy.wait_send()
        corr_copy.wait_send()


def local(initial, guess, velocity, heat_shape, rack_map, power, fan_mode):
    blocks, slabs = lax.axis_size("tm"), lax.axis_size("space")
    planes, ny, nz = initial.shape
    steps, racks = power.shape
    width = -(-racks // 128) * 128
    onehot = (rack_map[:, :, None] == lax.iota(jnp.int32, width)[None, None, :]).astype(jnp.float32)
    levels = jnp.pad(power.astype(jnp.float32), ((0, 0), (0, width - racks)))
    levels = jnp.broadcast_to(levels[:, :, None], (steps, width, nz))
    tall = ny + 2 * PAD
    vmem = pl.BlockSpec(memory_space=pltpu.VMEM)
    hbm = pl.BlockSpec(memory_space=pl.ANY)
    f32 = jnp.float32
    return pl.pallas_call(
        functools.partial(kernel, blocks, slabs),
        out_shape=jax.ShapeDtypeStruct((steps, planes, ny, nz), f32),
        in_specs=[pl.BlockSpec(memory_space=pltpu.SMEM), hbm, hbm, hbm, vmem, vmem, vmem],
        out_specs=vmem,
        scratch_shapes=[
            pltpu.VMEM((steps, planes + 2, ny, nz), f32),
            pltpu.VMEM((planes + 2, ny, nz), f32),
            pltpu.VMEM((planes + 2, ny, width), f32),
            pltpu.VMEM((2, planes + 4, tall, nz), f32),
            pltpu.VMEM((planes + 2, tall, nz), f32),
            pltpu.VMEM((planes + 4, tall, nz), f32),
            pltpu.VMEM((planes + 4, tall, nz), f32),
            pltpu.VMEM((planes, ny, nz), f32),
            pltpu.VMEM((planes, ny, nz), f32),
            pltpu.VMEM((planes, ny, nz), f32),
            pltpu.VMEM((velocity.shape[0], 3, planes + 2, ny, nz), f32),
            pltpu.SemaphoreType.DMA((2, 2, 2)),
            pltpu.SemaphoreType.DMA((2, 2, 2)),
            pltpu.SemaphoreType.DMA((2,)),
            pltpu.SemaphoreType.DMA((2,)),
            pltpu.SemaphoreType.DMA((2,)),
            pltpu.SemaphoreType.DMA((2,)),
            pltpu.SemaphoreType.DMA((2,)),
            pltpu.SemaphoreType.DMA((2,)),
            pltpu.SemaphoreType.DMA((2,)),
            pltpu.SemaphoreType.DMA((2,)),
            pltpu.SemaphoreType.DMA((2,)),
            pltpu.SemaphoreType.DMA((2,)),
            pltpu.SemaphoreType.DMA((5,)),
        ],
        compiler_params=pltpu.CompilerParams(
            collective_id=0, has_side_effects=True, vmem_limit_bytes=40 * 1024 * 1024
        ),
    )(fan_mode, initial, guess, velocity, heat_shape, onehot, levels)


def solution(mesh):
    placed = (
        P("space", None, None),
        P("tm", "space", None, None),
        P(None, None, "space", None, None),
        P("space", None, None),
        P("space", None),
        P("tm", None),
        P(),
    )
    return jax.shard_map(
        local, mesh=mesh, in_specs=placed, out_specs=P("tm", "space", None, None), check_vma=False
    )
```
